128 devices in a mesh: tm: 8 (over x_lo, z), space: 16 (over x_hi, y, core).
Axes of the slice: x: 4 (x_hi: 2, x_lo: 2; x = x_hi * 2 + x_lo), y: 4, z: 4, core: 2. Of those that a mesh axis runs over, the one named last changes fastest.
Arguments:
- query: bfloat16 [8, 1024, 4096], P('tm', 'space'), may hold values from -80 to 80
- key: bfloat16 [8, 1024, 4096], P('tm', 'space'), may hold values from -4 to 4
- value: bfloat16 [8, 1024, 4096], P('tm', 'space'), may hold values from -6 to 6
- widths: int32 [4, 8], replicated, may hold values from 0 to 7, as said below
Outputs:
- attended: bfloat16 [8, 1024, 4096], P('tm', 'space')
The draws below stay inside these ranges and needn't reach their ends.
Inputs may be any that keep to these rules, and one draw needn't show every extreme that they name: `widths`: some entry is 0 and another is 7.
All inputs are finite; a program needn't handle non-finite values.
Results may differ from the reference program's by a relative error of at most 0.0049.
Values may be sent and summed in bfloat16 or wider, within the bound.
No kernel may reach another device: no remote copies, remote signals or barrier semaphores. Data moves between devices by JAX's collectives and lax.ppermute only.
A program may use at most 192 MiB of HBM per device.

```python
import jax
import jax.numpy as jnp
from jax import lax

HEADS = 32
HEAD_DIM = 128
BLK = 128
FRAMES = 8
FRAME_TOK = 1024
FRAME_BLK = 8
LEVELS = 4


def shared_draw(key):
    shape = (FRAMES, FRAME_TOK, HEADS * HEAD_DIM)
    base_field = jnp.clip(jax.random.normal(jax.random.fold_in(key, 11), shape, jnp.float32), -4.0, 4.0)
    return base_field


def draw_key(key, part):
    base_field = shared_draw(key)
    return base_field.astype(jnp.bfloat16)


def draw_query(key, part):
    key = jax.random.fold_in(key, 2)
    shape = (FRAMES, FRAME_TOK, HEADS * HEAD_DIM)
    result = 2.0 * jnp.clip(jax.random.normal(key, shape, jnp.float32), -4.0, 4.0)
    return result.astype(jnp.bfloat16)


def draw_widths(key, part):
    key = jax.random.fold_in(key, 4)
    value_key, order_key = jax.random.split(key)
    entries = LEVELS * FRAME_BLK
    drawn = jax.random.randint(value_key, (entries,), 0, FRAME_BLK)
    order = jax.random.permutation(order_key, entries)
    drawn = drawn.at[order[0]].set(0)
    drawn = drawn.at[order[1]].set(FRAME_BLK - 1)
    return drawn.reshape(LEVELS, FRAME_BLK).astype(jnp.int32)


def block_scale(own_key, extent, cuts, least, high):
    gain, own = 1.0, jax.random.fold_in(own_key, 6)
    for position, blocks in cuts:
        draws = jnp.exp(jax.random.uniform(jax.random.fold_in(own, position), (blocks,), jnp.float32, least / len(cuts), high / len(cuts)))
        gain = gain * jnp.repeat(draws, extent[position] // blocks).reshape([-1 if axis == position else 1 for axis in range(len(extent))])
    return gain


def gaussian(own_key, dims, deviation, limit, shards=(), kind=jnp.bfloat16):
    values = jax.random.normal(own_key, dims, jnp.float32) * deviation
    if len(shards) > 0:
        values = block_scale(own_key, dims, shards, -0.22, 0.18) * values
    return jnp.clip(values, min=-limit, max=limit).astype(kind)


def setup_inputs(seed: int = 0) -> dict:
    seeds = jax.random.split(jax.random.key(seed), 5)
    query = draw_query(jax.random.fold_in(seeds[4], 71), 0)
    key = draw_key(jax.random.fold_in(seeds[4], 71), 0)
    value = gaussian(seeds[2], (FRAMES, FRAME_TOK, HEADS * HEAD_DIM), 1.0, 6.0, ((0, 8), (1, 16)))
    widths = draw_widths(jax.random.fold_in(seeds[4], 71), 0)
    return dict(query=query, key=key, value=value, widths=widths)


def reference(query, key, value, widths):
    shaped = (FRAMES, FRAME_TOK, HEADS, HEAD_DIM)
    queries = query.reshape(shaped)
    all_keys = jnp.transpose(key.reshape(FRAMES * FRAME_TOK, HEADS, HEAD_DIM), (1, 0, 2))
    all_values = jnp.transpose(value.reshape(FRAMES * FRAME_TOK, HEADS, HEAD_DIM), (1, 0, 2))
    token_block = jnp.arange(FRAME_TOK, dtype=jnp.int32) // BLK
    key_block = jnp.tile(token_block, FRAMES)
    key_frame = jnp.repeat(jnp.arange(FRAMES, dtype=jnp.int32), FRAME_TOK)
    row_widths = jnp.transpose(widths)[token_block]

    def one_frame(frame_index):
        distance = jnp.abs(key_frame - frame_index).astype(jnp.int32)
        key_level = jnp.zeros_like(distance)
        for level_index in range(LEVELS):
            key_level = key_level + (distance > 2 ** level_index).astype(jnp.int32)
        key_level = jnp.minimum(key_level, LEVELS - 1).astype(jnp.int32)
        pair_width = row_widths[:, key_level]
        key_limit = jnp.where(distance[None, :] == 0, FRAME_BLK, pair_width)
        allowed = jnp.abs(token_block[:, None] - key_block[None, :]) <= key_limit
        own_queries = jnp.transpose(queries[frame_index], (1, 0, 2))

        def one_head(operands):
            q_head, k_head, v_head = operands
            scores = jnp.dot(q_head, k_head.T, preferred_element_type=jnp.float32) * (HEAD_DIM ** -0.5)
            scores = jnp.where(allowed, scores, -jnp.inf)
            row_top = jnp.max(scores, axis=1, keepdims=True)
            exp_scores = jnp.exp(scores - row_top)
            weights = (exp_scores / jnp.sum(exp_scores, axis=1, keepdims=True)).astype(jnp.bfloat16)
            return jnp.dot(weights, v_head, preferred_element_type=jnp.float32).astype(jnp.bfloat16)

        head_out = lax.map(one_head, (own_queries, all_keys, all_values))
        return jnp.transpose(head_out, (1, 0, 2))

    result = lax.map(one_frame, jnp.arange(FRAMES, dtype=jnp.int32))
    return result.reshape(FRAMES, FRAME_TOK, HEADS * HEAD_DIM)
```

```python
import functools

import jax
import jax.numpy as jnp
from jax import lax
from jax.experimental import pallas as pl
from jax.experimental.pallas import tpu as pltpu
from jax.sharding import Mesh, PartitionSpec as P

HEADS = 32
DIM = 128
BLK = 128
LOG2E = 1.4426950408889634
SCALE = LOG2E * DIM ** -0.5
FRAMES = 8
BLOCKS = 8
BAND = 64
HALF = BAND // 2
TILE = BLOCKS * HALF
KEYS = BLOCKS * BAND
ROWS = FRAMES * TILE
OFF = -1e30
SAFE = 80.0
CHIPS = ("xl", "z1", "z0", "xh", "y")
NT = (((1,), (1,)), ((), ()))


def pack_kernel(q_ref, k_ref, v_ref, out_ref):
    for head in range(HEADS):
        cols = slice(head * DIM, (head + 1) * DIM)
        high, low = head // 8, head % 8
        keys, values = k_ref[:, cols], v_ref[:, cols]
        for half in range(2):
            dest = (high * 2 + half) * 8 + low
            out_ref[dest, 0:HALF, :] = q_ref[half * HALF:(half + 1) * HALF, cols]
            out_ref[dest, HALF:HALF + BAND, :] = keys
            out_ref[dest, HALF + BAND:, :] = values


def unpack_kernel(in_ref, out_ref):
    for head in range(HEADS):
        high, low = head // 8, head % 8
        for half in range(2):
            out_ref[half * HALF:(half + 1) * HALF, head * DIM:(head + 1) * DIM] = in_ref[(high * 2 + half) * 8 + low]


def fill_bias(w_ref, bias):
    block = lax.broadcasted_iota(jnp.int32, (1, KEYS), 1) // BAND
    bias[0] = jnp.zeros((BLOCKS, KEYS), jnp.float32)
    for level in range(4):
        for row in range(BLOCKS):
            near = jnp.abs(block - row) <= w_ref[level, row]
            bias[level + 1, row:row + 1, :] = jnp.where(near, 0.0, OFF)


def pattern(query_frame, key_frame):
    gap = jnp.abs(query_frame - key_frame)
    return (gap > 0).astype(jnp.int32) + (gap > 1).astype(jnp.int32) + (gap > 2).astype(jnp.int32) + (gap > 4).astype(jnp.int32)


def queries_of(q_ref, frame):
    return q_ref[pl.ds(frame * BLOCKS, BLOCKS), 0:HALF, :].reshape(TILE, DIM)


def keys_of(kv_ref, frame):
    return kv_ref[frame * BLOCKS:(frame + 1) * BLOCKS, HALF:HALF + BAND, :].reshape(KEYS, DIM)


def values_of(kv_ref, frame):
    return kv_ref[frame * BLOCKS:(frame + 1) * BLOCKS, HALF + BAND:, :].reshape(KEYS, DIM)


def scores_of(queries, keys, bias, query_frame, key_frame):
    scores = lax.dot_general(queries, keys, NT, preferred_element_type=jnp.float32) * SCALE
    rows = bias[pattern(query_frame, key_frame)]
    spread = jnp.broadcast_to(rows[:, None, :], (BLOCKS, HALF, KEYS)).reshape(TILE, KEYS)
    return scores + spread


def norm_top(ref, first, last):
    block = ref[:, first:last, :].astype(jnp.float32)
    return jnp.max(jnp.sum(block * block, axis=-1))


def attend_kernel(merge, w_ref, q_ref, kv_ref, *refs):
    if merge:
        before, top_before, out_ref, bias, shift = refs
    else:
        out_ref, shift, bias = refs
    fill_bias(w_ref, bias)
    bound = norm_top(q_ref, 0, HALF) * norm_top(kv_ref, HALF, HALF + BAND)
    wide = jnp.logical_not(bound * (SCALE * SCALE) <= SAFE * SAFE)
    if merge:
        wide = wide | (jnp.max(jnp.abs(top_before[...])) > 0.0)
    shift[...] = jnp.zeros((ROWS, DIM), jnp.float32)

    @pl.when(wide)
    def _():
        def tops(step, _):
            queries = queries_of(q_ref, step)
            rows = pl.ds(step * TILE, TILE)
            top = top_before[rows, :] if merge else jnp.full((TILE, DIM), OFF, jnp.float32)
            for frame in range(FRAMES):
                scores = scores_of(queries, keys_of(kv_ref, frame), bias, step, frame)
                top = jnp.maximum(top, jnp.max(scores, axis=1, keepdims=True))
            shift[rows, :] = top
            return 0

        lax.fori_loop(0, FRAMES, tops, 0)

    def body(step, _):
        queries = queries_of(q_ref, step)
        rows = pl.ds(step * TILE, TILE)
        top = shift[rows, :]
        lowered = jnp.concatenate([top] * (KEYS // DIM), axis=1)
        total = jnp.zeros((TILE, 2 * DIM), jnp.float32)
        for frame in range(FRAMES):
            scores = scores_of(queries, keys_of(kv_ref, frame), bias, step, frame)
            weights = jnp.exp2(scores - lowered).astype(jnp.bfloat16)
            values = jnp.concatenate([values_of(kv_ref, frame), jnp.ones((KEYS, DIM), jnp.bfloat16)], axis=1)
            total = total + jnp.dot(weights, values, preferred_element_type=jnp.float32)
        if merge:
            scale = jnp.exp2(top_before[rows, :] - top)
            old = before[rows, :]
            upper = total[:, :DIM] + old[:, :DIM] * scale
            lower = total[:, DIM:] + old[:, DIM:] * scale
            result = (upper / lower).astype(jnp.bfloat16)
            out_ref[pl.ds(step * BLOCKS, BLOCKS), :, :] = result.reshape(BLOCKS, HALF, DIM)
        else:
            out_ref[rows, :] = total
        return 0

    lax.fori_loop(0, FRAMES, body, 0)


def attend(widths, arrived, keyed, before=None):
    merge = before is not None
    vmem = pl.BlockSpec(memory_space=pltpu.VMEM)
    bias = pltpu.VMEM((5, BLOCKS, KEYS), jnp.float32)
    tops = jax.ShapeDtypeStruct((ROWS, DIM), jnp.float32)
    if merge:
        shape = jax.ShapeDtypeStruct((FRAMES * BLOCKS, HALF, DIM), jnp.bfloat16)
        scratch, specs = [bias, pltpu.VMEM((ROWS, DIM), jnp.float32)], vmem
    else:
        shape = [jax.ShapeDtypeStruct((ROWS, 2 * DIM), jnp.float32), tops]
        scratch, specs = [bias], [vmem, vmem]
    pairs = ROWS * FRAMES * KEYS
    return pl.pallas_call(
        functools.partial(attend_kernel, merge),
        out_shape=shape,
        in_specs=[pl.BlockSpec(memory_space=pltpu.SMEM)] + [vmem] * (4 if merge else 2),
        out_specs=specs,
        scratch_shapes=scratch,
        compiler_params=pltpu.CompilerParams(vmem_limit_bytes=50 << 20),
        cost_estimate=pl.CostEstimate(flops=pairs * DIM * 6, bytes_accessed=6 << 20, transcendentals=pairs),
    )(widths, arrived, keyed, *(before or ()))


def on_device(query, key, value, widths):
    vmem = pl.BlockSpec(memory_space=pltpu.VMEM)
    parcels = pl.pallas_call(
        pack_kernel,
        out_shape=jax.ShapeDtypeStruct((2 * HEADS, HALF + 2 * BAND, DIM), jnp.bfloat16),
        in_specs=[vmem] * 3,
        out_specs=vmem,
        compiler_params=pltpu.CompilerParams(vmem_limit_bytes=32 << 20),
        cost_estimate=pl.CostEstimate(flops=0, bytes_accessed=4 << 20, transcendentals=0),
    )(query[0], key[0], value[0])
    arrived = lax.all_to_all(parcels, CHIPS, split_axis=0, concat_axis=0, tiled=True)
    other = lax.ppermute(arrived, "c", [(0, 1), (1, 0)])
    before = attend(widths, arrived, arrived)
    result = attend(widths, arrived, other, before)
    returned = lax.all_to_all(result, CHIPS, split_axis=0, concat_axis=0, tiled=True)
    out = pl.pallas_call(
        unpack_kernel,
        out_shape=jax.ShapeDtypeStruct((BAND, HEADS * DIM), jnp.bfloat16),
        in_specs=[vmem],
        out_specs=vmem,
        compiler_params=pltpu.CompilerParams(vmem_limit_bytes=32 << 20),
        cost_estimate=pl.CostEstimate(flops=0, bytes_accessed=1 << 20, transcendentals=0),
    )(returned)
    return out[None]


def solution(mesh):
    fine = Mesh(mesh.devices.reshape(2, 2, 2, 2, 4, 2), CHIPS + ("c",))
    banded = P(("xl", "z1", "z0"), ("xh", "y", "c"), None)
    return jax.shard_map(
        on_device,
        mesh=fine,
        in_specs=(banded, banded, banded, P()),
        out_specs=banded,
        check_vma=False,
    )
```

```python
import functools

import jax
import jax.numpy as jnp
from jax import lax
from jax.experimental import pallas as pl
from jax.experimental.pallas import tpu as pltpu
from jax.sharding import Mesh, PartitionSpec as P

HEADS = 32
DIM = 128
BLOCKS = 8
BAND = 64
FRAMES = 8
NEAR = 4
SPAN = NEAR * BAND
TILE = 2 * SPAN
ROWS = FRAMES * SPAN
STEPS = ROWS // TILE
LOG2E = 1.4426950408889634
SCALE = LOG2E * DIM ** -0.5
OFF = -1e30
SAFE = 80.0
UNROLL = 8
CUT = 6
GROUP = ("xl", "z1", "z0", "y")
SWAP = [(0, 1), (1, 0)]
NT = (((1,), (1,)), ((), ()))
VMEM = pl.BlockSpec(memory_space=pltpu.VMEM)


def pack_kernel(q_ref, k_ref, v_ref, out_ref):
    for index, ref in enumerate((q_ref, k_ref, v_ref)):
        for head in range(HEADS):
            out_ref[head, index * BAND:(index + 1) * BAND, :] = ref[0, :, head * DIM:(head + 1) * DIM]


def unpack_kernel(in_ref, out_ref):
    for head in range(HEADS):
        out_ref[0, :, head * DIM:(head + 1) * DIM] = in_ref[head]


def fill_bias(w_ref, bias, side):
    place = lax.broadcasted_iota(jnp.int32, (1, SPAN), 1) // BAND
    for far in range(2):
        block = place + (1 - side if far else side) * NEAR
        bias[far, 0] = jnp.zeros((NEAR, SPAN), jnp.float32)
        for level in range(4):
            for row in range(NEAR):
                own = side * NEAR + row
                reach = jnp.abs(block - own) <= w_ref[level, own]
                bias[far, level + 1, row:row + 1, :] = jnp.where(reach, 0.0, OFF)


def pattern(query_frame, key_frame):
    gap = jnp.abs(query_frame - key_frame)
    return (gap > 0).astype(jnp.int32) + (gap > 1).astype(jnp.int32) + (gap > 2).astype(jnp.int32) + (gap > 4).astype(jnp.int32)


def norm_top(ref, first):
    top = jnp.zeros((TILE, DIM), jnp.float32)
    ones = jnp.ones((DIM, DIM), jnp.bfloat16)
    for place in range(ref.shape[0] // BLOCKS):
        block = ref[place * BLOCKS:(place + 1) * BLOCKS, first:first + BAND, :].reshape(TILE, DIM).astype(jnp.float32)
        top = jnp.maximum(top, jnp.dot((block * block).astype(jnp.bfloat16), ones, preferred_element_type=jnp.float32))
    return jnp.max(top) * 1.02


def attend_kernel(parts, first, last, *refs):
    count = len(parts)
    q_ref, kv_refs, refs = refs[0], refs[1:1 + count], refs[1 + count:]
    if first:
        w_ref, refs = refs[0], refs[1:]
    else:
        before, top_before, facts_before, bias, refs = *refs[:4], refs[4:]
    if last:
        out_ref, refs = refs[0], refs[1:]
    elif first:
        out_ref, top_out, facts_out, bias, refs = *refs[:4], refs[4:]
    else:
        out_ref, top_out, facts_out, refs = *refs[:3], refs[3:]
    older, shift, sem = refs
    if first:
        fill_bias(w_ref, bias, lax.axis_index("xh"))
        query_top, wide_before = norm_top(q_ref, 0), None
    else:
        query_top, wide_before = jnp.max(facts_before[0:1, :]), jnp.max(facts_before[1:2, :]) > 0.0
    key_top = 0.0
    for (base, _, _), kv_ref in zip(parts, kv_refs):
        key_top = jnp.maximum(key_top, norm_top(kv_ref, base))
    wide = jnp.logical_not(query_top * key_top * (SCALE * SCALE) <= SAFE * SAFE)
    if not first:
        wide = wide | wide_before
    if not last:
        facts_out[0:1, :] = jnp.full((1, DIM), query_top, jnp.float32)
        facts_out[1:2, :] = jnp.full((1, DIM), wide.astype(jnp.float32), jnp.float32)

    tiles = []
    for (base, far, frame), kv_ref in zip(parts, kv_refs):
        for slot in range(kv_ref.shape[0] // BLOCKS):
            tiles.append((kv_ref, base, far, slot, frame + 2 * slot))

    def queries_of(step):
        return q_ref[pl.ds(step * BLOCKS, BLOCKS), 0:BAND, :].reshape(TILE, DIM)

    def scores_of(queries, step, tile):
        kv_ref, base, far, slot, frame = tile
        keys = kv_ref[slot * BLOCKS:(slot + 1) * BLOCKS, base:base + BAND, :].reshape(TILE, DIM)
        scores = lax.dot_general(queries, keys, NT, preferred_element_type=jnp.float32) * SCALE
        bands = []
        for own in range(2):
            rows = jnp.concatenate([bias[far, pattern(2 * step + own, frame + other)] for other in range(2)], axis=1)
            bands.append(jnp.broadcast_to(rows[:, None, :], (NEAR, BAND, TILE)).reshape(SPAN, TILE))
        return scores + jnp.concatenate(bands, axis=0)

    def attended(step, shifted):
        queries = queries_of(step)
        rows = pl.ds(step * TILE, TILE)
        if shifted:
            lowered = jnp.concatenate([shift[rows, :]] * (TILE // DIM), axis=1)
        total = jnp.zeros((TILE, 2 * DIM), jnp.float32) if first or shifted else before[rows, :]
        for tile in tiles:
            kv_ref, base, _, slot, _ = tile
            scores = scores_of(queries, step, tile)
            weights = jnp.exp2(scores - lowered if shifted else scores).astype(jnp.bfloat16)
            values = kv_ref[slot * BLOCKS:(slot + 1) * BLOCKS, base + BAND:base + 2 * BAND, :].reshape(TILE, DIM)
            values = jnp.concatenate([values, jnp.ones((TILE, DIM), jnp.bfloat16)], axis=1)
            total = total + jnp.dot(weights, values, preferred_element_type=jnp.float32)
        if shifted and not first:
            scale = jnp.exp2(older[rows, :] - shift[rows, :])
            total = total + before[rows, :] * jnp.concatenate([scale, scale], axis=1)
        if last:
            result = (total[:, :DIM] / total[:, DIM:]).astype(jnp.bfloat16)
            out_ref[pl.ds(step * BLOCKS, BLOCKS), :, :] = result.reshape(BLOCKS, BAND, DIM)
        else:
            out_ref[rows, :] = total

    @pl.when(jnp.logical_not(wide))
    def _():
        unrolled = min(STEPS, max(1, UNROLL // len(tiles)))

        def body(group, _):
            for step in range(unrolled):
                attended(group * unrolled + step, False)
            return 0

        lax.fori_loop(0, STEPS // unrolled, body, 0)

    @pl.when(wide)
    def _():
        if first:
            older[...] = jnp.full((ROWS, DIM), OFF, jnp.float32)
        else:
            older[...] = jnp.zeros((ROWS, DIM), jnp.float32)

            @pl.when(wide_before)
            def _():
                copy = pltpu.make_async_copy(top_before, older, sem)
                copy.start()
                copy.wait()

        def body(step, _):
            queries = queries_of(step)
            rows = pl.ds(step * TILE, TILE)
            top = older[rows, :]
            for tile in tiles:
                top = jnp.maximum(top, jnp.max(scores_of(queries, step, tile), axis=1, keepdims=True))
            shift[rows, :] = top
            attended(step, True)
            return 0

        lax.fori_loop(0, STEPS, body, 0)
        if not last:
            copy = pltpu.make_async_copy(shift, top_out, sem)
            copy.start()
            copy.wait()


def attend(arrived, keyed, parts, widths=None, before=(), last=False):
    first = not before
    anywhere, scalars = pl.BlockSpec(memory_space=pl.ANY), pl.BlockSpec(memory_space=pltpu.SMEM)
    extra = [widths] if first else list(before)
    if last:
        shape, specs = jax.ShapeDtypeStruct((HEADS, BAND, DIM), jnp.bfloat16), VMEM
    else:
        shape = [
            jax.ShapeDtypeStruct((ROWS, 2 * DIM), jnp.float32),
            jax.ShapeDtypeStruct((ROWS, DIM), jnp.float32),
            jax.ShapeDtypeStruct((8, DIM), jnp.float32),
        ]
        specs = [VMEM, anywhere, VMEM]
        if first:
            shape.append(jax.ShapeDtypeStruct((2, 5, NEAR, SPAN), jnp.float32))
            specs.append(VMEM)
    pairs = ROWS * TILE * sum(array.shape[0] // BLOCKS for array in keyed)
    return pl.pallas_call(
        functools.partial(attend_kernel, parts, first, last),
        out_shape=shape,
        in_specs=[VMEM] * (1 + len(keyed)) + ([scalars] if first else [VMEM, anywhere, VMEM, VMEM]),
        out_specs=specs,
        scratch_shapes=[
            pltpu.VMEM((ROWS, DIM), jnp.float32),
            pltpu.VMEM((ROWS, DIM), jnp.float32),
            pltpu.SemaphoreType.DMA,
        ],
        compiler_params=pltpu.CompilerParams(vmem_limit_bytes=28 << 20),
        cost_estimate=pl.CostEstimate(flops=pairs * DIM * 8, bytes_accessed=6 << 20, transcendentals=pairs),
    )(arrived, *keyed, *extra)


def on_device(query, key, value, widths):
    parcels = pl.pallas_call(
        pack_kernel,
        out_shape=jax.ShapeDtypeStruct((HEADS, 3 * BAND, DIM), jnp.bfloat16),
        in_specs=[VMEM] * 3,
        out_specs=VMEM,
        compiler_params=pltpu.CompilerParams(vmem_limit_bytes=62 << 20),
        cost_estimate=pl.CostEstimate(flops=0, bytes_accessed=4 << 20, transcendentals=0),
    )(query, key, value)
    arrived = lax.all_to_all(parcels, GROUP, split_axis=0, concat_axis=0, tiled=True)
    own = arrived[:, BAND:, :]
    across_low, across_high = (lax.ppermute(part, "xh", SWAP) for part in (own[:CUT * NEAR], own[CUT * NEAR:]))
    beside = lax.ppermute(own, "c", SWAP)
    near, far_low, far_high = (0, 0, 0), (0, 1, 0), (0, 1, CUT)

    def after(state, array):
        return lax.optimization_barrier((tuple(state), array))

    *state, bias = attend(arrived, [arrived], [(BAND, 0, 0)], widths)

    def step(keyed, parts, state, last=False):
        return attend(arrived, keyed, parts, None, (*state, bias), last)

    state = step([beside], [near], state)
    state, across_low = after(state, across_low)
    fourth_low = lax.ppermute(across_low, "c", SWAP)
    state = step([across_low], [far_low], state)
    state = step([fourth_low], [far_low], state)
    state, across_high = after(state, across_high)
    fourth_high = lax.ppermute(across_high, "c", SWAP)
    state = step([across_high], [far_high], state)
    result = step([fourth_high], [far_high], state, True)
    returned = lax.all_to_all(result, GROUP, split_axis=0, concat_axis=0, tiled=True)
    return pl.pallas_call(
        unpack_kernel,
        out_shape=jax.ShapeDtypeStruct((1, BAND, HEADS * DIM), jnp.bfloat16),
        in_specs=[VMEM],
        out_specs=VMEM,
        compiler_params=pltpu.CompilerParams(vmem_limit_bytes=32 << 20),
        cost_estimate=pl.CostEstimate(flops=0, bytes_accessed=1 << 20, transcendentals=0),
    )(returned)


def solution(mesh):
    fine = Mesh(mesh.devices.reshape(2, 2, 2, 2, 4, 2), ("xl", "z1", "z0", "xh", "y", "c"))
    banded = P(("xl", "z1", "z0"), ("xh", "y", "c"), None)
    return jax.shard_map(
        on_device,
        mesh=fine,
        in_specs=(banded, banded, banded, P()),
        out_specs=banded,
        check_vma=False,
    )
```

```python
import functools

import jax
import jax.numpy as jnp
from jax import lax
from jax.experimental import pallas as pl
from jax.experimental.pallas import tpu as pltpu
from jax.sharding import Mesh, PartitionSpec as P

HEADS = 32
DIM = 128
BLOCKS = 8
BAND = 64
FRAMES = 8
NEAR = 4
SPAN = NEAR * BAND
TILE = 2 * SPAN
ROWS = FRAMES * SPAN
STEPS = ROWS // TILE
LOG2E = 1.4426950408889634
SCALE = LOG2E * DIM ** -0.5
OFF = -1e30
SAFE = 80.0
PAIR = 4
PARTS = 2
STRIP = BAND // PARTS
CUT = 3
GROUP = ("xl", "z1", "z0", "y")
SWAP = [(0, 1), (1, 0)]
NT = (((1,), (1,)), ((), ()))
VMEM = pl.BlockSpec(memory_space=pltpu.VMEM)


def pack_kernel(q_ref, k_ref, v_ref, out_ref, held, ready, came, left):
    pieces = [(index, part) for index in range(3) for part in range(PARTS)]
    arrivals, departures = [], []
    for index, part in pieces:
        rows = slice(part * STRIP, (part + 1) * STRIP)
        ref = (q_ref, k_ref, v_ref)[index]
        arrivals.append(pltpu.make_async_copy(ref.at[0, rows, :], held.at[index, rows, :], came.at[index, part]))
        arrivals[-1].start()
    for (index, part), arrival in zip(pieces, arrivals):
        arrival.wait()
        first = part * STRIP
        target = slice(index * BAND + first, index * BAND + first + STRIP)
        for head in range(HEADS):
            ready[head, target, :] = held[index, first:first + STRIP, head * DIM:(head + 1) * DIM]
        departures.append(pltpu.make_async_copy(ready.at[:, target, :], out_ref.at[:, target, :], left.at[index, part]))
        departures[-1].start()
    for departure in departures:
        departure.wait()


def unpack_kernel(in_ref, out_ref):
    for head in range(HEADS):
        out_ref[0, :, head * DIM:(head + 1) * DIM] = in_ref[head]


def fill_bias(w_ref, bias, side):
    place = lax.broadcasted_iota(jnp.int32, (1, SPAN), 1) // BAND
    for far in range(2):
        block = place + (1 - side if far else side) * NEAR
        bias[far, 0] = jnp.zeros((NEAR, SPAN), jnp.float32)
        for level in range(4):
            for row in range(NEAR):
                own = side * NEAR + row
                reach = jnp.abs(block - own) <= w_ref[level, own]
                bias[far, level + 1, row:row + 1, :] = jnp.where(reach, 0.0, OFF)


def pattern(query_frame, key_frame):
    gap = jnp.abs(query_frame - key_frame)
    return (gap > 0).astype(jnp.int32) + (gap > 1).astype(jnp.int32) + (gap > 2).astype(jnp.int32) + (gap > 4).astype(jnp.int32)


def norm_top(ref, first):
    top = jnp.zeros((SPAN, DIM), jnp.float32)
    ones = jnp.ones((DIM, DIM), jnp.bfloat16)
    for frame in range(ref.shape[0] // NEAR):
        block = ref[frame * NEAR:(frame + 1) * NEAR, first:first + BAND, :].reshape(SPAN, DIM).astype(jnp.float32)
        top = jnp.maximum(top, jnp.dot((block * block).astype(jnp.bfloat16), ones, preferred_element_type=jnp.float32))
    return jnp.max(top) * 1.02


def attend_kernel(parts, first, last, *refs):
    count = len(parts)
    q_ref, kv_refs, refs = refs[0], refs[1:1 + count], refs[1 + count:]
    if first:
        w_ref, refs = refs[0], refs[1:]
    else:
        before, top_before, facts_before, bias, refs = *refs[:4], refs[4:]
    if last:
        out_ref, refs = refs[0], refs[1:]
    elif first:
        out_ref, top_out, facts_out, bias, refs = *refs[:4], refs[4:]
    else:
        out_ref, top_out, facts_out, refs = *refs[:3], refs[3:]
    older, shift, sem = refs
    if first:
        fill_bias(w_ref, bias, lax.axis_index("xh"))
        query_top, wide_before = norm_top(q_ref, 0), None
    else:
        query_top, wide_before = jnp.max(facts_before[0:1, :]), jnp.max(facts_before[1:2, :]) > 0.0
    key_top = 0.0
    for (base, _, _), kv_ref in zip(parts, kv_refs):
        key_top = jnp.maximum(key_top, norm_top(kv_ref, base))
    wide = jnp.logical_not(query_top * key_top * (SCALE * SCALE) <= SAFE * SAFE)
    if not first:
        wide = wide | wide_before
    if not last:
        facts_out[0:1, :] = jnp.full((1, DIM), query_top, jnp.float32)
        facts_out[1:2, :] = jnp.full((1, DIM), wide.astype(jnp.float32), jnp.float32)

    tiles = []
    for (base, far, frame), kv_ref in zip(parts, kv_refs):
        count = kv_ref.shape[0] // NEAR
        for slot in range(0, count, 2):
            tiles.append((kv_ref, base, far, slot, min(2, count - slot), frame + slot))

    def cut(tile, first):
        kv_ref, _, _, slot, width, _ = tile
        return kv_ref[slot * NEAR:(slot + width) * NEAR, first:first + BAND, :].reshape(width * SPAN, DIM)

    def queries_of(step):
        return q_ref[pl.ds(step * BLOCKS, BLOCKS), 0:BAND, :].reshape(TILE, DIM)

    def scores_of(queries, step, tile):
        _, base, far, _, width, frame = tile
        keys = cut(tile, base)
        scores = lax.dot_general(queries, keys, NT, preferred_element_type=jnp.float32) * SCALE
        bands = []
        for own in range(2):
            rows = jnp.concatenate([bias[far, pattern(2 * step + own, frame + other)] for other in range(width)], axis=1)
            bands.append(jnp.broadcast_to(rows[:, None, :], (NEAR, BAND, width * SPAN)).reshape(SPAN, width * SPAN))
        return scores + jnp.concatenate(bands, axis=0)

    def attended(steps, shifted):
        queries = [queries_of(step) for step in steps]
        spans = [pl.ds(step * TILE, TILE) for step in steps]
        totals = [jnp.zeros((TILE, 2 * DIM), jnp.float32) if first or shifted else before[rows, :] for rows in spans]
        for tile in tiles:
            values = cut(tile, tile[1] + BAND)
            values = jnp.concatenate([values, jnp.ones(values.shape, jnp.bfloat16)], axis=1)
            for index, step in enumerate(steps):
                scores = scores_of(queries[index], step, tile)
                if shifted:
                    scores = scores - jnp.concatenate([shift[spans[index], :]] * (scores.shape[1] // DIM), axis=1)
                weights = jnp.exp2(scores).astype(jnp.bfloat16)
                totals[index] = totals[index] + jnp.dot(weights, values, preferred_element_type=jnp.float32)
        for step, rows, total in zip(steps, spans, totals):
            if shifted and not first:
                scale = jnp.exp2(older[rows, :] - shift[rows, :])
                total = total + before[rows, :] * jnp.concatenate([scale, scale], axis=1)
            if last:
                result = (total[:, :DIM] / total[:, DIM:]).astype(jnp.bfloat16)
                out_ref[pl.ds(step * BLOCKS, BLOCKS), :, :] = result.reshape(BLOCKS, BAND, DIM)
            else:
                out_ref[rows, :] = total

    @pl.when(jnp.logical_not(wide))
    def _():
        def body(group, _):
            attended([group * PAIR + step for step in range(PAIR)], False)
            return 0

        lax.fori_loop(0, STEPS // PAIR, body, 0)

    @pl.when(wide)
    def _():
        if first:
            older[...] = jnp.full((ROWS, DIM), OFF, jnp.float32)
        else:
            older[...] = jnp.zeros((ROWS, DIM), jnp.float32)

            @pl.when(wide_before)
            def _():
                copy = pltpu.make_async_copy(top_before, older, sem)
                copy.start()
                copy.wait()

        def body(step, _):
            queries = queries_of(step)
            rows = pl.ds(step * TILE, TILE)
            top = older[rows, :]
            for tile in tiles:
                top = jnp.maximum(top, jnp.max(scores_of(queries, step, tile), axis=1, keepdims=True))
            shift[rows, :] = top
            attended([step], True)
            return 0

        lax.fori_loop(0, STEPS, body, 0)
        if not last:
            copy = pltpu.make_async_copy(shift, top_out, sem)
            copy.start()
            copy.wait()


def attend(arrived, keyed, parts, widths=None, before=(), last=False):
    first = not before
    anywhere, scalars = pl.BlockSpec(memory_space=pl.ANY), pl.BlockSpec(memory_space=pltpu.SMEM)
    extra = [widths] if first else list(before)
    if last:
        shape, specs = jax.ShapeDtypeStruct((HEADS, BAND, DIM), jnp.bfloat16), VMEM
    else:
        shape = [
            jax.ShapeDtypeStruct((ROWS, 2 * DIM), jnp.float32),
            jax.ShapeDtypeStruct((ROWS, DIM), jnp.float32),
            jax.ShapeDtypeStruct((8, DIM), jnp.float32),
        ]
        specs = [VMEM, anywhere, VMEM]
        if first:
            shape.append(jax.ShapeDtypeStruct((2, 5, NEAR, SPAN), jnp.float32))
            specs.append(VMEM)
    pairs = ROWS * TILE * sum(array.shape[0] for array in keyed) // BLOCKS
    return pl.pallas_call(
        functools.partial(attend_kernel, parts, first, last),
        out_shape=shape,
        in_specs=[VMEM] * (1 + len(keyed)) + ([scalars] if first else [VMEM, anywhere, VMEM, VMEM]),
        out_specs=specs,
        scratch_shapes=[
            pltpu.VMEM((ROWS, DIM), jnp.float32),
            pltpu.VMEM((ROWS, DIM), jnp.float32),
            pltpu.SemaphoreType.DMA,
        ],
        compiler_params=pltpu.CompilerParams(vmem_limit_bytes=28 << 20),
        cost_estimate=pl.CostEstimate(flops=pairs * DIM * 8, bytes_accessed=6 << 20, transcendentals=pairs),
    )(arrived, *keyed, *extra)


def on_device(query, key, value, widths):
    parcels = pl.pallas_call(
        pack_kernel,
        out_shape=jax.ShapeDtypeStruct((HEADS, 3 * BAND, DIM), jnp.bfloat16),
        in_specs=[pl.BlockSpec(memory_space=pl.ANY)] * 3,
        out_specs=pl.BlockSpec(memory_space=pl.ANY),
        scratch_shapes=[
            pltpu.VMEM((3, BAND, HEADS * DIM), jnp.bfloat16),
            pltpu.VMEM((HEADS, 3 * BAND, DIM), jnp.bfloat16),
            pltpu.SemaphoreType.DMA((3, PARTS)),
            pltpu.SemaphoreType.DMA((3, PARTS)),
        ],
        compiler_params=pltpu.CompilerParams(vmem_limit_bytes=62 << 20),
        cost_estimate=pl.CostEstimate(flops=0, bytes_accessed=4 << 20, transcendentals=0),
    )(query, key, value)
    arrived = lax.all_to_all(parcels, GROUP, split_axis=0, concat_axis=0, tiled=True)
    own = arrived[:, BAND:, :]
    across_low, across_high = (lax.ppermute(part, "xh", SWAP) for part in (own[:CUT * NEAR], own[CUT * NEAR:]))
    beside = lax.ppermute(own, "c", SWAP)
    near, far_low, far_high = (0, 0, 0), (0, 1, 0), (0, 1, CUT)

    def after(state, array):
        return lax.optimization_barrier((tuple(state), array))

    *state, bias = attend(arrived, [arrived], [(BAND, 0, 0)], widths)

    def step(keyed, parts, state, last=False):
        return attend(arrived, keyed, parts, None, (*state, bias), last)

    state = step([beside], [near], state)
    state, across_low = after(state, across_low)
    fourth_low = lax.ppermute(across_low, "c", SWAP)
    state = step([across_low], [far_low], state)
    state = step([fourth_low], [far_low], state)
    state, across_high = after(state, across_high)
    fourth_high = lax.ppermute(across_high, "c", SWAP)
    state = step([across_high], [far_high], state)
    result = step([fourth_high], [far_high], state, True)
    returned = lax.all_to_all(result, GROUP, split_axis=0, concat_axis=0, tiled=True)
    return pl.pallas_call(
        unpack_kernel,
        out_shape=jax.ShapeDtypeStruct((1, BAND, HEADS * DIM), jnp.bfloat16),
        in_specs=[VMEM],
        out_specs=VMEM,
        compiler_params=pltpu.CompilerParams(vmem_limit_bytes=32 << 20),
        cost_estimate=pl.CostEstimate(flops=0, bytes_accessed=1 << 20, transcendentals=0),
    )(returned)


def solution(mesh):
    fine = Mesh(mesh.devices.reshape(2, 2, 2, 2, 4, 2), ("xl", "z1", "z0", "xh", "y", "c"))
    banded = P(("xl", "z1", "z0"), ("xh", "y", "c"), None)
    return jax.shard_map(
        on_device,
        mesh=fine,
        in_specs=(banded, banded, banded, P()),
        out_specs=banded,
        check_vma=False,
    )
```

```python
import functools

import jax
import jax.numpy as jnp
from jax import lax
from jax.experimental import pallas as pl
from jax.experimental.pallas import tpu as pltpu
from jax.sharding import Mesh, PartitionSpec as P

HEADS = 32
DIM = 128
BLOCKS = 8
BAND = 64
FRAMES = 8
NEAR = 4
SPAN = NEAR * BAND
TILE = 2 * SPAN
ROWS = FRAMES * SPAN
STEPS = ROWS // TILE
LOG2E = 1.4426950408889634
SCALE = LOG2E * DIM ** -0.5
OFF = -1e30
SAFE = 80.0
PAIR = 4
PARTS = 2
STRIP = BAND // PARTS
CUT = 3
GROUP = ("z1", "z0", "xl", "y")
SWAP = [(0, 1), (1, 0)]
NT = (((1,), (1,)), ((), ()))
VMEM = pl.BlockSpec(memory_space=pltpu.VMEM)


def pack_kernel(q_ref, k_ref, v_ref, out_ref, held, ready, came, left):
    pieces = [(index, part) for index in range(3) for part in range(PARTS)]
    arrivals, departures = [], []
    for index, part in pieces:
        rows = slice(part * STRIP, (part + 1) * STRIP)
        ref = (q_ref, k_ref, v_ref)[index]
        arrivals.append(pltpu.make_async_copy(ref.at[0, rows, :], held.at[index, rows, :], came.at[index, part]))
        arrivals[-1].start()
    for (index, part), arrival in zip(pieces, arrivals):
        arrival.wait()
        first = part * STRIP
        target = slice(index * BAND + first, index * BAND + first + STRIP)
        for head in range(HEADS):
            ready[head, target, :] = held[index, first:first + STRIP, head * DIM:(head + 1) * DIM]
        departures.append(pltpu.make_async_copy(ready.at[:, target, :], out_ref.at[:, target, :], left.at[index, part]))
        departures[-1].start()
    for departure in departures:
        departure.wait()


def unpack_kernel(in_ref, out_ref):
    for head in range(HEADS):
        out_ref[0, :, head * DIM:(head + 1) * DIM] = in_ref[head]


def fill_bias(w_ref, bias, side):
    place = lax.broadcasted_iota(jnp.int32, (1, SPAN), 1) // BAND
    for far in range(2):
        block = place + (1 - side if far else side) * NEAR
        bias[far, 0] = jnp.zeros((NEAR, SPAN), jnp.float32)
        for level in range(4):
            for row in range(NEAR):
                own = side * NEAR + row
                reach = jnp.abs(block - own) <= w_ref[level, own]
                bias[far, level + 1, row:row + 1, :] = jnp.where(reach, 0.0, OFF)


def pattern(query_frame, key_frame):
    gap = jnp.abs(query_frame - key_frame)
    return (gap > 0).astype(jnp.int32) + (gap > 1).astype(jnp.int32) + (gap > 2).astype(jnp.int32) + (gap > 4).astype(jnp.int32)


def norm_top(ref, first):
    top = jnp.zeros((SPAN, DIM), jnp.float32)
    ones = jnp.ones((DIM, DIM), jnp.bfloat16)
    for frame in range(ref.shape[0] // NEAR):
        block = ref[frame * NEAR:(frame + 1) * NEAR, first:first + BAND, :].reshape(SPAN, DIM).astype(jnp.float32)
        top = jnp.maximum(top, jnp.dot((block * block).astype(jnp.bfloat16), ones, preferred_element_type=jnp.float32))
    return jnp.max(top) * 1.02


def attend_kernel(parts, first, last, *refs):
    count = len(parts)
    q_ref, kv_refs, refs = refs[0], refs[1:1 + count], refs[1 + count:]
    if first:
        w_ref, refs = refs[0], refs[1:]
    else:
        before, top_before, facts_before, bias, refs = *refs[:4], refs[4:]
    if last:
        out_ref, refs = refs[0], refs[1:]
    elif first:
        out_ref, top_out, facts_out, bias, refs = *refs[:4], refs[4:]
    else:
        out_ref, top_out, facts_out, refs = *refs[:3], refs[3:]
    older, shift, sem = refs
    if first:
        fill_bias(w_ref, bias, lax.axis_index("xh"))
        query_top, wide_before = norm_top(q_ref, 0), None
    else:
        query_top, wide_before = jnp.max(facts_before[0:1, :]), jnp.max(facts_before[1:2, :]) > 0.0
    key_top = 0.0
    for (base, _, _), kv_ref in zip(parts, kv_refs):
        key_top = jnp.maximum(key_top, norm_top(kv_ref, base))
    wide = jnp.logical_not(query_top * key_top * (SCALE * SCALE) <= SAFE * SAFE)
    if not first:
        wide = wide | wide_before
    if not last:
        facts_out[0:1, :] = jnp.full((1, DIM), query_top, jnp.float32)
        facts_out[1:2, :] = jnp.full((1, DIM), wide.astype(jnp.float32), jnp.float32)

    tiles = []
    for (base, far, frame), kv_ref in zip(parts, kv_refs):
        count = kv_ref.shape[0] // NEAR
        for slot in range(0, count, 2):
            tiles.append((kv_ref, base, far, slot, min(2, count - slot), frame + slot))

    def cut(tile, first):
        kv_ref, _, _, slot, width, _ = tile
        return kv_ref[slot * NEAR:(slot + width) * NEAR, first:first + BAND, :].reshape(width * SPAN, DIM)

    def queries_of(step):
        return q_ref[pl.ds(step * BLOCKS, BLOCKS), 0:BAND, :].reshape(TILE, DIM)

    def scores_of(queries, step, tile):
        _, base, far, _, width, frame = tile
        keys = cut(tile, base)
        scores = lax.dot_general(queries, keys, NT, preferred_element_type=jnp.float32) * SCALE
        bands = []
        for own in range(2):
            rows = jnp.concatenate([bias[far, pattern(own * NEAR + step, (frame + other) % 2 * NEAR + (frame + other) // 2)] for other in range(width)], axis=1)
            bands.append(jnp.broadcast_to(rows[:, None, :], (NEAR, BAND, width * SPAN)).reshape(SPAN, width * SPAN))
        return scores + jnp.concatenate(bands, axis=0)

    def attended(steps, shifted):
        queries = [queries_of(step) for step in steps]
        spans = [pl.ds(step * TILE, TILE) for step in steps]
        totals = [jnp.zeros((TILE, 2 * DIM), jnp.float32) if first or shifted else before[rows, :] for rows in spans]
        for tile in tiles:
            values = cut(tile, tile[1] + BAND)
            values = jnp.concatenate([values, jnp.ones(values.shape, jnp.bfloat16)], axis=1)
            for index, step in enumerate(steps):
                scores = scores_of(queries[index], step, tile)
                if shifted:
                    scores = scores - jnp.concatenate([shift[spans[index], :]] * (scores.shape[1] // DIM), axis=1)
                weights = jnp.exp2(scores).astype(jnp.bfloat16)
                totals[index] = totals[index] + jnp.dot(weights, values, preferred_element_type=jnp.float32)
        for step, rows, total in zip(steps, spans, totals):
            if shifted and not first:
                scale = jnp.exp2(older[rows, :] - shift[rows, :])
                total = total + before[rows, :] * jnp.concatenate([scale, scale], axis=1)
            if last:
                result = (total[:, :DIM] / total[:, DIM:]).astype(jnp.bfloat16)
                out_ref[pl.ds(step * BLOCKS, BLOCKS), :, :] = result.reshape(BLOCKS, BAND, DIM)
            else:
                out_ref[rows, :] = total

    @pl.when(jnp.logical_not(wide))
    def _():
        def body(group, _):
            attended([group * PAIR + step for step in range(PAIR)], False)
            return 0

        lax.fori_loop(0, STEPS // PAIR, body, 0)

    @pl.when(wide)
    def _():
        if first:
            older[...] = jnp.full((ROWS, DIM), OFF, jnp.float32)
        else:
            older[...] = jnp.zeros((ROWS, DIM), jnp.float32)

            @pl.when(wide_before)
            def _():
                copy = pltpu.make_async_copy(top_before, older, sem)
                copy.start()
                copy.wait()

        def body(step, _):
            queries = queries_of(step)
            rows = pl.ds(step * TILE, TILE)
            top = older[rows, :]
            for tile in tiles:
                top = jnp.maximum(top, jnp.max(scores_of(queries, step, tile), axis=1, keepdims=True))
            shift[rows, :] = top
            attended([step], True)
            return 0

        lax.fori_loop(0, STEPS, body, 0)
        if not last:
            copy = pltpu.make_async_copy(shift, top_out, sem)
            copy.start()
            copy.wait()


def attend(arrived, keyed, parts, widths=None, before=(), last=False):
    first = not before
    anywhere, scalars = pl.BlockSpec(memory_space=pl.ANY), pl.BlockSpec(memory_space=pltpu.SMEM)
    extra = [widths] if first else list(before)
    if last:
        shape, specs = jax.ShapeDtypeStruct((HEADS, BAND, DIM), jnp.bfloat16), VMEM
    else:
        shape = [
            jax.ShapeDtypeStruct((ROWS, 2 * DIM), jnp.float32),
            jax.ShapeDtypeStruct((ROWS, DIM), jnp.float32),
            jax.ShapeDtypeStruct((8, DIM), jnp.float32),
        ]
        specs = [VMEM, anywhere, VMEM]
        if first:
            shape.append(jax.ShapeDtypeStruct((2, 5, NEAR, SPAN), jnp.float32))
            specs.append(VMEM)
    pairs = ROWS * TILE * sum(array.shape[0] for array in keyed) // BLOCKS
    return pl.pallas_call(
        functools.partial(attend_kernel, parts, first, last),
        out_shape=shape,
        in_specs=[VMEM] * (1 + len(keyed)) + ([scalars] if first else [VMEM, anywhere, VMEM, VMEM]),
        out_specs=specs,
        scratch_shapes=[
            pltpu.VMEM((ROWS, DIM), jnp.float32),
            pltpu.VMEM((ROWS, DIM), jnp.float32),
            pltpu.SemaphoreType.DMA,
        ],
        compiler_params=pltpu.CompilerParams(vmem_limit_bytes=28 << 20),
        cost_estimate=pl.CostEstimate(flops=pairs * DIM * 8, bytes_accessed=6 << 20, transcendentals=pairs),
    )(arrived, *keyed, *extra)


def on_device(query, key, value, widths):
    parcels = pl.pallas_call(
        pack_kernel,
        out_shape=jax.ShapeDtypeStruct((HEADS, 3 * BAND, DIM), jnp.bfloat16),
        in_specs=[pl.BlockSpec(memory_space=pl.ANY)] * 3,
        out_specs=pl.BlockSpec(memory_space=pl.ANY),
        scratch_shapes=[
            pltpu.VMEM((3, BAND, HEADS * DIM), jnp.bfloat16),
            pltpu.VMEM((HEADS, 3 * BAND, DIM), jnp.bfloat16),
            pltpu.SemaphoreType.DMA((3, PARTS)),
            pltpu.SemaphoreType.DMA((3, PARTS)),
        ],
        compiler_params=pltpu.CompilerParams(vmem_limit_bytes=62 << 20),
        cost_estimate=pl.CostEstimate(flops=0, bytes_accessed=4 << 20, transcendentals=0),
    )(query, key, value)
    arrived = lax.all_to_all(parcels, GROUP, split_axis=0, concat_axis=0, tiled=True)
    own = arrived[:, BAND:, :]
    across_low, across_high = (lax.ppermute(part, "xh", SWAP) for part in (own[:CUT * NEAR], own[CUT * NEAR:]))
    beside = lax.ppermute(own, "c", SWAP)
    near, far_low, far_high = (0, 0, 0), (0, 1, 0), (0, 1, CUT)

    def after(state, array):
        return lax.optimization_barrier((tuple(state), array))

    *state, bias = attend(arrived, [arrived], [(BAND, 0, 0)], widths)

    def step(keyed, parts, state, last=False):
        return attend(arrived, keyed, parts, None, (*state, bias), last)

    state = step([beside], [near], state)
    state, across_low = after(state, across_low)
    fourth_low = lax.ppermute(across_low, "c", SWAP)
    state = step([across_low], [far_low], state)
    state = step([fourth_low], [far_low], state)
    state, across_high = after(state, across_high)
    fourth_high = lax.ppermute(across_high, "c", SWAP)
    state = step([across_high], [far_high], state)
    result = step([fourth_high], [far_high], state, True)
    returned = lax.all_to_all(result, GROUP, split_axis=0, concat_axis=0, tiled=True)
    return pl.pallas_call(
        unpack_kernel,
        out_shape=jax.ShapeDtypeStruct((1, BAND, HEADS * DIM), jnp.bfloat16),
        in_specs=[VMEM],
        out_specs=VMEM,
        compiler_params=pltpu.CompilerParams(vmem_limit_bytes=32 << 20),
        cost_estimate=pl.CostEstimate(flops=0, bytes_accessed=1 << 20, transcendentals=0),
    )(returned)


def solution(mesh):
    fine = Mesh(mesh.devices.reshape(2, 2, 2, 2, 4, 2), ("xl", "z1", "z0", "xh", "y", "c"))
    banded = P(("xl", "z1", "z0"), ("xh", "y", "c"), None)
    return jax.shard_map(
        on_device,
        mesh=fine,
        in_specs=(banded, banded, banded, P()),
        out_specs=banded,
        check_vma=False,
    )
```

```python
import functools

import jax
import jax.numpy as jnp
from jax import lax
from jax.experimental import pallas as pl
from jax.experimental.pallas import tpu as pltpu
from jax.sharding import Mesh, PartitionSpec as P

HEADS = 32
DIM = 128
BLOCKS = 8
BAND = 64
FRAMES = 8
NEAR = 4
SPAN = NEAR * BAND
TILE = 2 * SPAN
ROWS = FRAMES * SPAN
STEPS = ROWS // TILE
LOG2E = 1.4426950408889634
SCALE = LOG2E * DIM ** -0.5
OFF = -1e30
SAFE = 80.0
PAIR = 4
PARTS = 2
STRIP = BAND // PARTS
CUT = 3
GROUP = ("xl", "z1", "z0", "y")
SWAP = [(0, 1), (1, 0)]
NT = (((1,), (1,)), ((), ()))
VMEM = pl.BlockSpec(memory_space=pltpu.VMEM)


def pack_kernel(q_ref, k_ref, v_ref, out_ref, held, ready, came, left):
    pieces = [(index, part) for index in range(3) for part in range(PARTS)]
    arrivals, departures = [], []
    for index, part in pieces:
        rows = slice(part * STRIP, (part + 1) * STRIP)
        ref = (q_ref, k_ref, v_ref)[index]
        arrivals.append(pltpu.make_async_copy(ref.at[0, rows, :], held.at[index, rows, :], came.at[index, part]))
        arrivals[-1].start()
    for (index, part), arrival in zip(pieces, arrivals):
        arrival.wait()
        first = part * STRIP
        target = slice(index * BAND + first, index * BAND + first + STRIP)
        for head in range(HEADS):
            ready[head, target, :] = held[index, first:first + STRIP, head * DIM:(head + 1) * DIM]
        departures.append(pltpu.make_async_copy(ready.at[:, target, :], out_ref.at[:, target, :], left.at[index, part]))
        departures[-1].start()
    for departure in departures:
        departure.wait()


def unpack_kernel(in_ref, out_ref):
    for head in range(HEADS):
        out_ref[0, :, head * DIM:(head + 1) * DIM] = in_ref[head]


def fill_bias(w_ref, bias, side):
    place = lax.broadcasted_iota(jnp.int32, (1, SPAN), 1) // BAND
    for far in range(2):
        block = place + (1 - side if far else side) * NEAR
        bias[far, 0] = jnp.zeros((NEAR, SPAN), jnp.float32)
        for level in range(4):
            for row in range(NEAR):
                own = side * NEAR + row
                reach = jnp.abs(block - own) <= w_ref[level, own]
                bias[far, level + 1, row:row + 1, :] = jnp.where(reach, 0.0, OFF)


def pattern(query_frame, key_frame):
    gap = jnp.abs(query_frame - key_frame)
    return (gap > 0).astype(jnp.int32) + (gap > 1).astype(jnp.int32) + (gap > 2).astype(jnp.int32) + (gap > 4).astype(jnp.int32)


def norm_top(ref, first):
    top = jnp.zeros((SPAN, DIM), jnp.float32)
    ones = jnp.ones((DIM, DIM), jnp.bfloat16)
    for frame in range(ref.shape[0] // NEAR):
        block = ref[frame * NEAR:(frame + 1) * NEAR, first:first + BAND, :].reshape(SPAN, DIM).astype(jnp.float32)
        top = jnp.maximum(top, jnp.dot((block * block).astype(jnp.bfloat16), ones, preferred_element_type=jnp.float32))
    return jnp.max(top) * 1.02


def attend_kernel(parts, first, last, *refs):
    count = len(parts)
    q_ref, kv_refs, refs = refs[0], refs[1:1 + count], refs[1 + count:]
    if first:
        w_ref, refs = refs[0], refs[1:]
    else:
        before, top_before, facts_before, bias, refs = *refs[:4], refs[4:]
    if last:
        out_ref, refs = refs[0], refs[1:]
    elif first:
        out_ref, top_out, facts_out, bias, refs = *refs[:4], refs[4:]
    else:
        out_ref, top_out, facts_out, refs = *refs[:3], refs[3:]
    older, shift, sem = refs
    if first:
        fill_bias(w_ref, bias, lax.axis_index("xh"))
        query_top, wide_before = norm_top(q_ref, 0), None
    else:
        query_top, wide_before = jnp.max(facts_before[0:1, :]), jnp.max(facts_before[1:2, :]) > 0.0
    key_top = 0.0
    for (base, _, _), kv_ref in zip(parts, kv_refs):
        key_top = jnp.maximum(key_top, norm_top(kv_ref, base))
    wide = jnp.logical_not(query_top * key_top * (SCALE * SCALE) <= SAFE * SAFE)
    if not first:
        wide = wide | wide_before
    if not last:
        facts_out[0:1, :] = jnp.full((1, DIM), query_top, jnp.float32)
        facts_out[1:2, :] = jnp.full((1, DIM), wide.astype(jnp.float32), jnp.float32)

    tiles = []
    for (base, far, frame), kv_ref in zip(parts, kv_refs):
        count = kv_ref.shape[0] // NEAR
        slot = 0
        while slot < count:
            width = 3 if (count - slot) % 2 else 2
            tiles.append((kv_ref, base, far, slot, width, frame + slot))
            slot += width

    def cut(tile, first):
        kv_ref, _, _, slot, width, _ = tile
        return kv_ref[slot * NEAR:(slot + width) * NEAR, first:first + BAND, :].reshape(width * SPAN, DIM)

    def queries_of(step):
        return q_ref[pl.ds(step * BLOCKS, BLOCKS), 0:BAND, :].reshape(TILE, DIM)

    def scores_of(queries, step, tile):
        _, base, far, _, width, frame = tile
        keys = cut(tile, base)
        scores = lax.dot_general(queries, keys, NT, preferred_element_type=jnp.float32) * SCALE
        bands = []
        for own in range(2):
            rows = jnp.concatenate([bias[far, pattern(2 * step + own, frame + other)] for other in range(width)], axis=1)
            bands.append(jnp.broadcast_to(rows[:, None, :], (NEAR, BAND, width * SPAN)).reshape(SPAN, width * SPAN))
        return scores + jnp.concatenate(bands, axis=0)

    def attended(steps, shifted):
        queries = [queries_of(step) for step in steps]
        spans = [pl.ds(step * TILE, TILE) for step in steps]
        totals = [jnp.zeros((TILE, 2 * DIM), jnp.float32) if first or shifted else before[rows, :] for rows in spans]
        for tile in tiles:
            values = cut(tile, tile[1] + BAND)
            values = jnp.concatenate([values, jnp.ones(values.shape, jnp.bfloat16)], axis=1)
            for index, step in enumerate(steps):
                scores = scores_of(queries[index], step, tile)
                if shifted:
                    scores = scores - jnp.concatenate([shift[spans[index], :]] * (scores.shape[1] // DIM), axis=1)
                weights = jnp.exp2(scores).astype(jnp.bfloat16)
                totals[index] = totals[index] + jnp.dot(weights, values, preferred_element_type=jnp.float32)
        for step, rows, total in zip(steps, spans, totals):
            if shifted and not first:
                scale = jnp.exp2(older[rows, :] - shift[rows, :])
                total = total + before[rows, :] * jnp.concatenate([scale, scale], axis=1)
            if last:
                result = (total[:, :DIM] / total[:, DIM:]).astype(jnp.bfloat16)
                out_ref[pl.ds(step * BLOCKS, BLOCKS), :, :] = result.reshape(BLOCKS, BAND, DIM)
            else:
                out_ref[rows, :] = total

    @pl.when(jnp.logical_not(wide))
    def _():
        def body(group, _):
            attended([group * PAIR + step for step in range(PAIR)], False)
            return 0

        lax.fori_loop(0, STEPS // PAIR, body, 0)

    @pl.when(wide)
    def _():
        if first:
            older[...] = jnp.full((ROWS, DIM), OFF, jnp.float32)
        else:
            older[...] = jnp.zeros((ROWS, DIM), jnp.float32)

            @pl.when(wide_before)
            def _():
                copy = pltpu.make_async_copy(top_before, older, sem)
                copy.start()
                copy.wait()

        def body(step, _):
            queries = queries_of(step)
            rows = pl.ds(step * TILE, TILE)
            top = older[rows, :]
            for tile in tiles:
                top = jnp.maximum(top, jnp.max(scores_of(queries, step, tile), axis=1, keepdims=True))
            shift[rows, :] = top
            attended([step], True)
            return 0

        lax.fori_loop(0, STEPS, body, 0)
        if not last:
            copy = pltpu.make_async_copy(shift, top_out, sem)
            copy.start()
            copy.wait()


def attend(arrived, keyed, parts, widths=None, before=(), last=False):
    first = not before
    anywhere, scalars = pl.BlockSpec(memory_space=pl.ANY), pl.BlockSpec(memory_space=pltpu.SMEM)
    extra = [widths] if first else list(before)
    if last:
        shape, specs = jax.ShapeDtypeStruct((HEADS, BAND, DIM), jnp.bfloat16), VMEM
    else:
        shape = [
            jax.ShapeDtypeStruct((ROWS, 2 * DIM), jnp.float32),
            jax.ShapeDtypeStruct((ROWS, DIM), jnp.float32),
            jax.ShapeDtypeStruct((8, DIM), jnp.float32),
        ]
        specs = [VMEM, anywhere, VMEM]
        if first:
            shape.append(jax.ShapeDtypeStruct((2, 5, NEAR, SPAN), jnp.float32))
            specs.append(VMEM)
    pairs = ROWS * TILE * sum(array.shape[0] for array in keyed) // BLOCKS
    return pl.pallas_call(
        functools.partial(attend_kernel, parts, first, last),
        out_shape=shape,
        in_specs=[VMEM] * (1 + len(keyed)) + ([scalars] if first else [VMEM, anywhere, VMEM, VMEM]),
        out_specs=specs,
        scratch_shapes=[
            pltpu.VMEM((ROWS, DIM), jnp.float32),
            pltpu.VMEM((ROWS, DIM), jnp.float32),
            pltpu.SemaphoreType.DMA,
        ],
        compiler_params=pltpu.CompilerParams(vmem_limit_bytes=28 << 20),
        cost_estimate=pl.CostEstimate(flops=pairs * DIM * 8, bytes_accessed=6 << 20, transcendentals=pairs),
    )(arrived, *keyed, *extra)


def on_device(query, key, value, widths):
    parcels = pl.pallas_call(
        pack_kernel,
        out_shape=jax.ShapeDtypeStruct((HEADS, 3 * BAND, DIM), jnp.bfloat16),
        in_specs=[pl.BlockSpec(memory_space=pl.ANY)] * 3,
        out_specs=pl.BlockSpec(memory_space=pl.ANY),
        scratch_shapes=[
            pltpu.VMEM((3, BAND, HEADS * DIM), jnp.bfloat16),
            pltpu.VMEM((HEADS, 3 * BAND, DIM), jnp.bfloat16),
            pltpu.SemaphoreType.DMA((3, PARTS)),
            pltpu.SemaphoreType.DMA((3, PARTS)),
        ],
        compiler_params=pltpu.CompilerParams(vmem_limit_bytes=62 << 20),
        cost_estimate=pl.CostEstimate(flops=0, bytes_accessed=4 << 20, transcendentals=0),
    )(query, key, value)
    arrived = lax.all_to_all(parcels, GROUP, split_axis=0, concat_axis=0, tiled=True)
    own = arrived[:, BAND:, :]
    across_low, across_high = (lax.ppermute(part, "xh", SWAP) for part in (own[:CUT * NEAR], own[CUT * NEAR:]))
    beside = lax.ppermute(own, "c", SWAP)
    near, far_low, far_high = (0, 0, 0), (0, 1, 0), (0, 1, CUT)

    def after(state, array):
        return lax.optimization_barrier((tuple(state), array))

    *state, bias = attend(arrived, [arrived], [(BAND, 0, 0)], widths)

    def step(keyed, parts, state, last=False):
        return attend(arrived, keyed, parts, None, (*state, bias), last)

    state = step([beside], [near], state)
    state, across_low = after(state, across_low)
    fourth_low = lax.ppermute(across_low, "c", SWAP)
    state = step([across_low], [far_low], state)
    state = step([fourth_low], [far_low], state)
    state, across_high = after(state, across_high)
    fourth_high = lax.ppermute(across_high, "c", SWAP)
    state = step([across_high], [far_high], state)
    result = step([fourth_high], [far_high], state, True)
    returned = lax.all_to_all(result, GROUP, split_axis=0, concat_axis=0, tiled=True)
    return pl.pallas_call(
        unpack_kernel,
        out_shape=jax.ShapeDtypeStruct((1, BAND, HEADS * DIM), jnp.bfloat16),
        in_specs=[VMEM],
        out_specs=VMEM,
        compiler_params=pltpu.CompilerParams(vmem_limit_bytes=32 << 20),
        cost_estimate=pl.CostEstimate(flops=0, bytes_accessed=1 << 20, transcendentals=0),
    )(returned)


def solution(mesh):
    fine = Mesh(mesh.devices.reshape(2, 2, 2, 2, 4, 2), ("xl", "z1", "z0", "xh", "y", "c"))
    banded = P(("xl", "z1", "z0"), ("xh", "y", "c"), None)
    return jax.shard_map(
        on_device,
        mesh=fine,
        in_specs=(banded, banded, banded, P()),
        out_specs=banded,
        check_vma=False,
    )
```
